32 devices in a mesh: ctx: 8 (over y, x, core), fsdp: 4 (over z).
Axes of the slice: x: 2, y: 2, z: 4, core: 2. Of those that a mesh axis runs over, the one named last changes fastest.
Arguments:
- hidden_in: bfloat16 [4096, 1152], P(('ctx', 'fsdp')), may hold values from -6 to 6
- attention_gain: bfloat16 [1152], P('fsdp'), may hold values from 0.5 to 1.5
- query_weight: bfloat16 [1152, 1152], P('fsdp'), may hold values from -0.1875 to 0.1875
- key_weight: bfloat16 [1152, 384], P('fsdp'), may hold values from -0.1875 to 0.1875
- value_weight: bfloat16 [1152, 384], P('fsdp'), may hold values from -0.1875 to 0.1875
- out_weight: bfloat16 [1152, 1152], P('fsdp'), may hold values from -1.5 to 1.5
- feed_gain: bfloat16 [1152], P('fsdp'), may hold values from 0.5 to 1.5
- gate_weight: bfloat16 [1152, 3072], P('fsdp'), may hold values from -0.1875 to 0.1875
- up_weight: bfloat16 [1152, 3072], P('fsdp'), may hold values from -0.1875 to 0.1875
- down_weight: bfloat16 [3072, 1152], P('fsdp'), may hold values from -0.109375 to 0.109375
- teacher: bfloat16 [4096, 1152], P(('ctx', 'fsdp')), may hold values from -6 to 6
- valid_mask: int32 [4096], P(('ctx', 'fsdp')), may hold values from 0 to 1, as said below
- doc_starts: int32 [8], replicated, may hold values from 0 to 4095, as said below
Outputs:
- grad_input: float32 [4096, 1152], P(('ctx', 'fsdp'))
- grad_attention_gain: float32 [1152], P('fsdp')
- grad_query_weight: float32 [1152, 1152], P('fsdp')
- grad_key_weight: float32 [1152, 384], P('fsdp')
- grad_value_weight: float32 [1152, 384], P('fsdp')
- grad_out_weight: float32 [1152, 1152], P('fsdp')
- grad_feed_gain: float32 [1152], P('fsdp')
- grad_gate_weight: float32 [1152, 3072], P('fsdp')
- grad_up_weight: float32 [1152, 3072], P('fsdp')
- grad_down_weight: float32 [3072, 1152], P('fsdp')
The draws below stay inside these ranges and needn't reach their ends.
Inputs may be any that keep to these rules, and one draw needn't show every extreme that they name: `doc_starts`: entry 0 is 0 and the entries rise strictly. `valid_mask`: row 0 holds 1.
All inputs are finite; a program needn't handle non-finite values.
Results may differ from the reference program's by a relative error of at most 0.022.
Values may be sent and summed in bfloat16 or wider, within the bound.
A program may use at most 320 MiB of HBM per device.

```python
import jax
import jax.numpy as jnp
from jax import lax

D = 1152
HQ = 18
HK = 6
HD = 64
FF = 3072
ROWS = 64
DOCS = 8
TOKENS = 4096
N_CTX = 8
N_FSDP = 4


def draw_valid_mask(key, part):
    key = jax.random.fold_in(key, 11)
    row_index = jnp.arange(TOKENS, dtype=jnp.int32)
    device_slot = row_index // (2 * ROWS)
    slot_count = TOKENS // (2 * ROWS)
    limit = 200 + 700 * device_slot // slot_count
    picked = jax.random.randint(key, (TOKENS,), 0, 1000)
    valid = jnp.where(picked < limit, 1, 0)
    return jnp.where(row_index == 0, 1, valid).astype(jnp.int32)


def draw_doc_starts(key, part):
    key = jax.random.fold_in(key, 23)
    first_key, rest_key = jax.random.split(key)
    lowest = TOKENS // 2 + TOKENS // 8
    second_start = jax.random.randint(first_key, (), lowest, lowest + TOKENS // 8)
    spacing = (TOKENS - second_start) // (DOCS - 1)
    offsets = jax.random.randint(rest_key, (DOCS - 2,), 0, spacing)
    later = second_start + spacing * jnp.arange(1, DOCS - 1, dtype=jnp.int32) + offsets
    return jnp.concatenate([jnp.zeros((1,), jnp.int32), second_start.reshape(1).astype(jnp.int32), later.astype(jnp.int32)]).astype(jnp.int32)


def levels(rng, extent, shards, low, top_value):
    level, own = 1.0, jax.random.fold_in(rng, 6)
    for dim, parts in shards:
        heights = jnp.exp(jax.random.uniform(jax.random.fold_in(own, dim), (parts,), jnp.float32, low / len(shards), top_value / len(shards)))
        level = level * jnp.repeat(heights, extent[dim] // parts).reshape([-1 if axis == dim else 1 for axis in range(len(extent))])
    return level


def scatter_about(stream_key, extent, scale, reach, cuts=(), held_as=jnp.bfloat16):
    gain = levels(stream_key, extent, cuts, -0.22, 0.18) if cuts else 1.0
    values = jax.random.normal(stream_key, extent, jnp.float32) * scale * gain
    return jnp.minimum(jnp.maximum(values, -reach), reach).astype(held_as)


def setup_inputs(seed: int = 0) -> dict:
    splits = jax.random.split(jax.random.key(seed), 14)
    return {
        "hidden_in": scatter_about(splits[0], (TOKENS, D), 1.0, 6.0, ((0, 32),)),
        "attention_gain": jnp.clip(1.0 + 0.1 * jax.random.normal(splits[1], (D,), jnp.float32), 0.5, 1.5).astype(jnp.bfloat16),
        "query_weight": scatter_about(splits[2], (D, HQ * HD), D ** -0.5, 0.1875, ((0, 4),)),
        "key_weight": scatter_about(splits[3], (D, HK * HD), D ** -0.5, 0.1875, ((0, 4),)),
        "value_weight": scatter_about(splits[4], (D, HK * HD), D ** -0.5, 0.1875, ((0, 4),)),
        "out_weight": scatter_about(splits[5], (HQ * HD, D), 16 ** -0.5, 1.5, ((0, 4),)),
        "feed_gain": jnp.clip(1.0 + 0.1 * jax.random.normal(splits[6], (D,), jnp.float32), 0.5, 1.5).astype(jnp.bfloat16),
        "gate_weight": scatter_about(splits[7], (D, FF), D ** -0.5, 0.1875, ((0, 4),)),
        "up_weight": scatter_about(splits[8], (D, FF), D ** -0.5, 0.1875, ((0, 4),)),
        "down_weight": scatter_about(splits[9], (FF, D), FF ** -0.5, 0.109375, ((0, 4),)),
        "teacher": scatter_about(splits[10], (TOKENS, D), 1.0, 6.0, ((0, 32),)),
        "valid_mask": draw_valid_mask(jax.random.fold_in(splits[13], 71), 0),
        "doc_starts": draw_doc_starts(jax.random.fold_in(splits[13], 71), 0),
    }


epsilon = 1e-05
rope_base = 10000.0
masked_score = -1e+30

@jax.custom_vjp
def low(v):
    return lax.optimization_barrier(v.astype(jnp.bfloat16)).astype(jnp.float32)

@jax.custom_vjp
def low_back(v):
    return v

def low_keep(v):
    return (low(v), None)

def low_pass(kept, grad):
    return (grad,)

def back_keep(v):
    return (v, None)

def back_low(kept, grad):
    return (low(grad),)
low.defvjp(low_keep, low_pass)
low_back.defvjp(back_keep, back_low)

def rotate(values, places, head_count, direction):
    half_size = HD // 2
    frequency = rope_base ** (-2.0 * jnp.arange(half_size, dtype=jnp.float32) / HD)
    angles = places.astype(jnp.float32)[:, None] * frequency[None, :]
    cosine = jnp.cos(angles)[:, None, :]
    sine = direction * jnp.sin(angles)[:, None, :]
    shaped = values.reshape(values.shape[0], head_count, HD)
    first_half = shaped[..., :half_size]
    second_half = shaped[..., half_size:]
    turned = jnp.concatenate([first_half * cosine - second_half * sine, second_half * cosine + first_half * sine], axis=-1)
    return turned.reshape(values.shape[0], head_count * HD)

def sequence_place(row_index, row_count, ctx_count, fsdp_count):
    device_slot = row_index // row_count
    within = row_index % row_count
    half_rows = row_count // 2
    ctx_slot = device_slot // fsdp_count
    fsdp_slot = device_slot % fsdp_count
    slab_index = jnp.where(within < half_rows, ctx_slot, 2 * ctx_count - 1 - ctx_slot)
    return (slab_index * (fsdp_count * half_rows) + fsdp_slot * half_rows + within % half_rows).astype(jnp.int32)

def product(left_side, right_side):
    return jnp.dot(left_side, right_side, precision=lax.Precision.HIGHEST)

def rms_norm(values, gain_vector):
    inverse = lax.rsqrt(lax.optimization_barrier(jnp.mean(values * values, axis=-1, keepdims=True)) + epsilon)
    return values * inverse * gain_vector

def reference(hidden_in, attention_gain, query_weight, key_weight, value_weight, out_weight, feed_gain, gate_weight, up_weight, down_weight, teacher, valid_mask, doc_starts):
    row_count = 2 * ROWS
    places = sequence_place(jnp.arange(TOKENS, dtype=jnp.int32), row_count, N_CTX, N_FSDP)
    segments = lax.optimization_barrier(jnp.sum((doc_starts[None, :] <= places[:, None]).astype(jnp.int32), axis=1)) - 1
    valid = valid_mask.astype(jnp.float32)
    count_all = jnp.sum(valid)
    target = teacher.astype(jnp.float32)
    block_size = min(512, TOKENS)
    block_count = TOKENS // block_size
    head_group = HQ // HK

    def attention(queries, keys, values):
        key_heads = keys.reshape(TOKENS, HK, HD).transpose(1, 0, 2)
        value_heads = values.reshape(TOKENS, HK, HD).transpose(1, 0, 2)

        def one_block(sliced):
            query_block, place_block, segment_block = sliced
            allowed = (segment_block[:, None] == segments[None, :]) & (places[None, :] <= place_block[:, None])
            query_heads = query_block.reshape(block_size, HK, head_group, HD).transpose(1, 2, 0, 3)

            def one_group(grouped):
                group_queries, group_keys, group_values = grouped
                products = jnp.einsum('jqd,kd->jqk', group_queries, group_keys, precision=lax.Precision.HIGHEST)
                scores = jnp.where(allowed[None], 0.125 * low_back(products), masked_score)
                shifted = scores - lax.optimization_barrier(jnp.max(scores, axis=-1, keepdims=True))
                exponent = jnp.exp(shifted)
                probs = exponent / lax.optimization_barrier(jnp.sum(exponent, axis=-1, keepdims=True))
                return jnp.einsum('jqk,kd->jqd', low(probs), group_values, precision=lax.Precision.HIGHEST)
            outputs = lax.map(jax.checkpoint(one_group), (query_heads, key_heads, value_heads))
            return outputs.transpose(2, 0, 1, 3).reshape(block_size, HQ * HD)
        results = lax.map(jax.checkpoint(one_block), (queries.reshape(block_count, block_size, HQ * HD), places.reshape(block_count, block_size), segments.reshape(block_count, block_size)))
        return results.reshape(TOKENS, HQ * HD)

    def forward(hidden, gain_one, query_matrix, key_matrix, value_matrix, out_matrix, gain_two, gate_matrix, up_matrix, down_matrix):
        normed = low(rms_norm(hidden, gain_one))
        query_pre = low_back(product(normed, query_matrix))
        key_pre = low_back(product(normed, key_matrix))
        value_pre = low_back(product(normed, value_matrix))
        queries = low(rotate(query_pre, places, HQ, 1.0))
        keys = low(rotate(key_pre, places, HK, 1.0))
        values = low(value_pre)
        attended = low(low_back(attention(queries, keys, values)))
        middle = hidden + low_back(product(attended, out_matrix))
        normed_two = low(rms_norm(middle, gain_two))
        gate_pre = low_back(product(normed_two, gate_matrix))
        up_pre = low_back(product(normed_two, up_matrix))
        inner = low(gate_pre * jax.nn.sigmoid(gate_pre) * up_pre)
        final = middle + low_back(product(inner, down_matrix))
        mismatch = final - target
        return TOKENS / (2.0 * count_all) * jnp.sum(valid[:, None] * mismatch * mismatch)
    floats = tuple((item.astype(jnp.float32) for item in (hidden_in, attention_gain, query_weight, key_weight, value_weight, out_weight, feed_gain, gate_weight, up_weight, down_weight)))
    loss, pullback = jax.vjp(forward, *floats)
    grads = pullback(jnp.ones_like(loss))
    return (grads[0], grads[1], grads[2], grads[3], grads[4], grads[5], grads[6], grads[7], grads[8], grads[9])
```

```python
import functools

import jax
import jax.numpy as jnp
from jax import lax
from jax.experimental import pallas as pl
from jax.experimental.pallas import tpu as pltpu
from jax.sharding import PartitionSpec as P

HQ = 18
HK = 6
HD = 64
TENSOR = 8
GROUPS = HK // 2
STACK = HQ // HK
QCOLS = HQ * HD // 2
KCOLS = HK * HD // 2
PACKED = 1024
GAIN_LANE = QCOLS + 2 * KCOLS - (PACKED - 128)
WIDE = 640

epsilon = 1e-05
rope_base = 10000.0
masked_score = -1e30
LOG2E = 1.4426950408889634
MESH = pl.DeviceIdType.MESH
BF = jnp.bfloat16
F32 = jnp.float32


def flip(index, mask):
    result, bit = index, 1
    while bit <= mask:
        if mask & bit:
            result = result + bit - 2 * bit * lax.rem(index // bit, 2)
        bit *= 2
    return result


def dot(left, right):
    return jnp.dot(left, right, preferred_element_type=F32)


def dot_t(left, right):
    return lax.dot_general(left, right, (((1,), (1,)), ((), ())), preferred_element_type=F32)


def t_dot(left, right):
    return lax.dot_general(left, right, (((0,), (0,)), ((), ())), preferred_element_type=F32)


def remote(src, dst, send_sem, recv_sem, device):
    return pltpu.make_async_remote_copy(
        src_ref=src,
        dst_ref=dst,
        send_sem=send_sem,
        recv_sem=recv_sem,
        device_id=device,
        device_id_type=MESH,
    )


def enter(devices):
    barrier = pltpu.get_barrier_semaphore()
    for device in devices:
        pl.semaphore_signal(barrier, inc=1, device_id=device, device_id_type=MESH)
    pl.semaphore_wait(barrier, len(devices))


class Where:
    def __init__(self, n_ctx, n_fsdp):
        self.n_ctx, self.n_fsdp = n_ctx, n_fsdp
        self.chips = n_ctx // 2
        self.share = TENSOR // 2
        self.c = lax.axis_index("ctx")
        self.z = lax.axis_index("fsdp")
        self.h = lax.rem(self.c, 2)
        self.p = self.c // 2
        self.t = lax.rem(self.c, TENSOR)
        self.s = lax.rem(self.p, self.share)
        self.base = self.p - self.s
        self.partner = (self.c + 1 - 2 * self.h, self.z)

    def chip(self, k):
        return flip(self.p, k)

    def peer(self, k):
        return (2 * flip(self.p, k) + self.h, self.z)

    def line(self, d):
        return (self.c, flip(self.z, d))


def lane_iota(shape):
    return lax.broadcasted_iota(jnp.int32, shape, len(shape) - 1)


def row_iota(shape):
    return lax.broadcasted_iota(jnp.int32, shape, len(shape) - 2)


def low_lanes(shape):
    return lane_iota(shape) < HD


def turn(tile, cosine, sine_signed):
    first = lax.rem(lane_iota(tile.shape), HD) < HD // 2
    swapped = jnp.where(
        first, pltpu.roll(tile, 128 - HD // 2, 1), pltpu.roll(tile, HD // 2, 1)
    )
    return tile * cosine + swapped * sine_signed


def place_of(where, half, chip, lane_or_row, fsdp_slot):
    core = lax.shift_right_logical(lax.bitwise_and(lane_or_row, 127), 6)
    within = lax.bitwise_and(lane_or_row, 63)
    slot = 2 * chip + core
    slab = slot + half * (2 * where.n_ctx - 1 - 2 * slot)
    return slab * (where.n_fsdp * 64) + fsdp_slot * 64 + within


def bias_of(where, starts_ref, query_half, key_half, key_chip):
    keys = where.n_fsdp * 128
    rows = row_iota((128, 1))
    place_q = place_of(where, query_half, where.p, rows, where.z)
    start_q = jnp.zeros((128, 1), jnp.int32)
    for d in range(starts_ref.shape[0]):
        begin = starts_ref[d]
        start_q = jnp.where(place_q >= begin, begin, start_q)
    lanes = lane_iota((1, keys))
    place_k = place_of(where, key_half, key_chip, lanes, lax.shift_right_logical(lanes, 7))
    allowed = (place_k <= place_q) & (place_k >= start_q)
    return jnp.where(allowed, 0.0, masked_score)


def fill_bias(where, starts_ref, bias):
    chips = where.chips
    for k in range(chips):
        chip = where.chip(k)
        high = (chip >= where.p).astype(jnp.int32)
        bias[2 * k] = bias_of(where, starts_ref, 1, 0, chip)
        bias[2 * k + 1] = bias_of(where, starts_ref, high, high, chip)
    bias[2 * chips] = bias_of(where, starts_ref, 0, 0, where.p)


def forward_kernel(
    n_ctx,
    n_fsdp,
    x_ref,
    w_ref,
    cos_ref,
    sin_ref,
    valid_ref,
    starts_ref,
    ob_ref,
    lse_ref,
    qs_ref,
    kv_ref,
    wf_ref,
    n1_ref,
    gains_ref,
    count_ref,
    x2,
    bias,
    top,
    total,
    acc,
    cnt_s,
    cnt_r,
    pair_ss,
    pair_rs,
    wz_ss,
    wz_rs,
    wp_ss,
    wp_rs,
    kz_ss,
    kz_rs,
    kp_ss,
    kp_rs,
    cp_ss,
    cp_rs,
):
    me = Where(n_ctx, n_fsdp)
    chips, share = me.chips, me.share
    rows = x_ref.shape[0]
    depth = w_ref.shape[0]
    width = x_ref.shape[1]
    piece = PACKED // share
    enter(
        [me.partner]
        + [me.line(d) for d in range(1, n_fsdp)]
        + [me.peer(k) for k in range(1, chips)]
    )
    own_cols = pl.ds(pl.multiple_of(me.s * piece, piece), piece)
    own_rows = pl.ds(pl.multiple_of(me.z * depth, 16), depth)
    sends = []

    def start(copy):
        copy.start()
        sends.append(copy)
        return copy

    wz = {}
    for d in range(1, n_fsdp):
        wz[d] = start(
            remote(
                w_ref.at[:, own_cols],
                wf_ref.at[own_rows, own_cols],
                wz_ss.at[d],
                wz_rs.at[d],
                me.line(d),
            )
        )
    x_copy = start(remote(x_ref, x2.at[me.h], pair_ss.at[0], pair_rs.at[0], me.partner))
    cnt_s[0] = jnp.full((8, 128), jnp.sum(valid_ref[...].astype(F32)), F32)
    c_copy = start(remote(cnt_s.at[0], cnt_r.at[0], pair_ss.at[1], pair_rs.at[1], me.partner))
    wf_ref[own_rows, :] = w_ref[...]
    x2[me.h] = x_ref[...]

    wp = {}
    for d in range(1, n_fsdp):
        wz[d].wait_recv()
        slot_rows = pl.ds(pl.multiple_of(flip(me.z, d) * depth, 16), depth)
        for k in range(1, share):
            wp[d, k] = start(
                remote(
                    wf_ref.at[slot_rows, own_cols],
                    wf_ref.at[slot_rows, own_cols],
                    wp_ss.at[d, k],
                    wp_rs.at[d, k],
                    me.peer(k),
                )
            )
    c_copy.wait_recv()
    cnt_s[1] = cnt_s[0] + cnt_r[0]
    cz = [
        start(remote(cnt_s.at[1], cnt_r.at[d], kz_ss.at[n_fsdp + d], kz_rs.at[n_fsdp + d], me.line(d)))
        for d in range(1, n_fsdp)
    ]
    fill_bias(me, starts_ref, bias)
    for copy in cz:
        copy.wait_recv()
    line_count = cnt_s[1]
    for d in range(1, n_fsdp):
        line_count = line_count + cnt_r[d]
    cnt_s[2] = line_count
    cp = [
        start(remote(cnt_s.at[2], cnt_r.at[n_fsdp + k], cp_ss.at[k], cp_rs.at[k], me.peer(k)))
        for k in range(1, chips)
    ]
    x_copy.wait_recv()
    for d in range(1, n_fsdp):
        for k in range(1, share):
            wp[d, k].wait_recv()

    pick = (lane_iota((8, 128)) == GAIN_LANE + row_iota((8, 128))).astype(BF)
    gains_ref[...] = dot_t(pick, wf_ref[:, PACKED - 128 :])
    gain = gains_ref[0:1]
    for core in range(2):
        x = x2[core].astype(F32)
        inverse = lax.rsqrt(jnp.mean(x * x, axis=-1, keepdims=True) + epsilon)
        n1_ref[core] = (x * inverse * gain).astype(BF)
    normed = n1_ref[...].reshape(2 * rows, width)
    cosine, sine = cos_ref[...], sin_ref[...]
    shape = (2 * rows, 128)
    low = low_lanes(shape)
    part = dot(normed, wf_ref[:, 512:])
    turned = [turn(part[:, 128 * i : 128 * (i + 1)], cosine, sine) for i in range(2)]
    last_query = jnp.where(low, turned[0], 0.0).astype(BF)
    raw = [part[:, 256:384], part[:, 384:512]]
    keys = [pltpu.roll(turned[0], HD, 1), turned[1], pltpu.roll(turned[1], HD, 1)]
    vals = [pltpu.roll(raw[0], HD, 1), raw[0], pltpu.roll(raw[1], HD, 1)]
    own_keys = pl.ds(pl.multiple_of(me.z * 128, 128), 128)
    for g in range(GROUPS):
        block = jnp.where(low, keys[g], vals[g]).astype(BF)
        for half in range(2):
            kv_ref[g, half, me.p, own_keys, :] = jnp.concatenate(
                [
                    block[core * rows + half * 64 : core * rows + half * 64 + 64]
                    for core in range(2)
                ],
                axis=0,
            )

    def kv_at(chip, slot):
        return kv_ref.at[:, :, chip, pl.ds(pl.multiple_of(slot * 128, 128), 128), :]

    kz = {}
    for d in range(1, n_fsdp):
        kz[d] = start(remote(kv_at(me.p, me.z), kv_at(me.p, me.z), kz_ss.at[d], kz_rs.at[d], me.line(d)))
    kp = {}

    def pass_on(d):
        slot = flip(me.z, d)
        for k in range(1, chips):
            kp[d, k] = start(
                remote(kv_at(me.p, slot), kv_at(me.p, slot), kp_ss.at[d, k], kp_rs.at[d, k], me.peer(k))
            )

    pass_on(0)
    part = dot(normed, wf_ref[:, :512])
    for head in range(GROUPS * STACK):
        g, j = head // STACK, head % STACK
        if head == GROUPS * STACK - 1:
            query = last_query
        else:
            tile = turn(part[:, 128 * (head // 2) : 128 * (head // 2 + 1)], cosine, sine)
            if head % 2:
                tile = pltpu.roll(tile, HD, 1)
            query = jnp.where(low, tile, 0.0).astype(BF)
        for half in range(2):
            qs_ref[g, half, j * 128 : (j + 1) * 128, :] = jnp.concatenate(
                [
                    query[core * rows + half * 64 : core * rows + half * 64 + 64]
                    for core in range(2)
                ],
                axis=0,
            )
    for d in range(1, n_fsdp):
        kz[d].wait_recv()
        pass_on(d)

    top[...] = jnp.full(top.shape, 2 * masked_score, F32)
    total[...] = jnp.zeros(total.shape, F32)
    acc[...] = jnp.zeros(acc.shape, F32)
    stacked = STACK * 128
    n_keys = n_fsdp * 128

    def chunk(query_half, key_half, chip, bias_index):
        def group(g, unused):
            kv = kv_ref[g, key_half, chip]
            scores = dot_t(qs_ref[g, query_half], kv) * (0.125 * LOG2E)
            scores = (scores.reshape(STACK, 128, n_keys) + bias[bias_index][None]).reshape(
                stacked, n_keys
            )
            old = top[g, query_half]
            new = jnp.maximum(old, jnp.max(scores, axis=-1, keepdims=True))
            factor = jnp.exp2(old - new)
            weights = jnp.exp2(scores - new)
            total[g, query_half] = total[g, query_half] * factor + jnp.sum(
                weights, axis=-1, keepdims=True
            )
            acc[g, query_half] = acc[g, query_half] * factor + dot(weights.astype(BF), kv)
            top[g, query_half] = new
            return unused

        lax.fori_loop(0, GROUPS, group, 0)

    for k in range(chips):
        chip = me.chip(k)
        high = (chip >= me.p).astype(jnp.int32)
        if k:
            for d in range(n_fsdp):
                kp[d, k].wait_recv()
        chunk(1, 0, chip, 2 * k)
        chunk(high, high, chip, 2 * k + 1)
        if k == 0:
            chunk(0, 0, chip, 2 * chips)
    low_half = low_lanes((128, 128))
    for half in range(2):
        outs = []
        for g in range(GROUPS):
            summed = total[g, half]
            out = acc[g, half] / summed
            lse_ref[g, half] = jnp.broadcast_to(
                top[g, half] + jnp.log(summed) * LOG2E, (stacked, 128)
            )
            outs += [out[128 * j : 128 * (j + 1)] for j in range(STACK)]
        outs.append(jnp.zeros((128, 128), F32))
        for i in range(WIDE // 128):
            tile = jnp.where(low_half, pltpu.roll(outs[2 * i], HD, 1), outs[2 * i + 1]).astype(BF)
            for core in range(2):
                ob_ref[core, half * 64 : half * 64 + 64, 128 * i : 128 * (i + 1)] = tile[
                    core * 64 : core * 64 + 64
                ]
    count = cnt_s[2]
    for k in range(1, chips):
        cp[k - 1].wait_recv()
        count = count + cnt_r[n_fsdp + k]
    count_ref[...] = count
    for copy in sends:
        copy.wait_send()


def forward_call(n_ctx, n_fsdp, x, w, cosine, sine, valid, starts):
    rows, width = x.shape
    chips, share = n_ctx // 2, TENSOR // 2
    keys = n_fsdp * 128
    stacked = STACK * 128
    vmem = pl.BlockSpec(memory_space=pltpu.VMEM)
    dma = pltpu.SemaphoreType.DMA
    outs = (
        jax.ShapeDtypeStruct((2, rows, WIDE), BF),
        jax.ShapeDtypeStruct((GROUPS, 2, stacked, 128), F32),
        jax.ShapeDtypeStruct((GROUPS, 2, stacked, 128), BF),
        jax.ShapeDtypeStruct((GROUPS, 2, chips, keys, 128), BF),
        jax.ShapeDtypeStruct((width, PACKED), BF),
        jax.ShapeDtypeStruct((2, rows, width), BF),
        jax.ShapeDtypeStruct((8, width), F32),
        jax.ShapeDtypeStruct((8, 128), F32),
    )
    return pl.pallas_call(
        functools.partial(forward_kernel, n_ctx, n_fsdp),
        out_shape=outs,
        in_specs=[vmem] * 5 + [pl.BlockSpec(memory_space=pltpu.SMEM)],
        out_specs=(vmem,) * len(outs),
        scratch_shapes=[
            pltpu.VMEM((2, rows, width), BF),
            pltpu.VMEM((2 * chips + 1, 128, keys), F32),
            pltpu.VMEM((GROUPS, 2, stacked, 1), F32),
            pltpu.VMEM((GROUPS, 2, stacked, 1), F32),
            pltpu.VMEM((GROUPS, 2, stacked, 128), F32),
            pltpu.VMEM((3, 8, 128), F32),
            pltpu.VMEM((n_fsdp + chips, 8, 128), F32),
            dma((2,)),
            dma((2,)),
            dma((n_fsdp,)),
            dma((n_fsdp,)),
            dma((n_fsdp, share)),
            dma((n_fsdp, share)),
            dma((2 * n_fsdp,)),
            dma((2 * n_fsdp,)),
            dma((n_fsdp, chips)),
            dma((n_fsdp, chips)),
            dma((chips,)),
            dma((chips,)),
        ],
        compiler_params=pltpu.CompilerParams(
            collective_id=1, has_side_effects=True, vmem_limit_bytes=60 * 2**20
        ),
        cost_estimate=pl.CostEstimate(
            flops=4 * 10**9, bytes_accessed=20 * 2**20, transcendentals=6 * 10**6
        ),
        name="attention_forward",
    )(x, w, cosine, sine, valid, starts)


class Plane:
    def __init__(self, where, start):
        self.me, self.start = where, start

    def gather_start(self, own, everything, sems):
        me = self.me
        pair_ss, pair_rs, peer_ss, peer_rs, on_ss, on_rs = sems
        slot = everything.at[me.t]
        copies = {0: self.start(remote(own, slot, pair_ss, pair_rs, me.partner))}
        for k in range(1, me.share):
            copies[k] = self.start(remote(own, slot, peer_ss.at[k], peer_rs.at[k], me.peer(k)))
        return copies

    def pass_on(self, k, copies, everything, sems):
        me = self.me
        on_ss, on_rs = sems[4:]
        copies[k].wait_recv()
        slot = everything.at[lax.rem(2 * me.chip(k) + me.h, TENSOR)]
        return self.start(remote(slot, slot, on_ss.at[k], on_rs.at[k], me.partner))


def feed_kernel(
    n_ctx,
    n_fsdp,
    x_ref,
    ob_ref,
    wo_ref,
    wgu_ref,
    wd_ref,
    gain_ref,
    teacher_ref,
    valid_ref,
    count_ref,
    gm_ref,
    dob_ref,
    gwo_ref,
    gwgu_ref,
    gwd_ref,
    ggain_ref,
    mix,
    mix_in,
    middle,
    n2,
    n2_all,
    wd,
    gate_s,
    up_s,
    inner_s,
    dgu_s,
    wide,
    keep,
    pair_out,
    pair_in,
    peer_out,
    peer_in,
    dy_s,
    dyb,
    dyb_all,
    dhb_all,
    pair_ss,
    pair_rs,
    g_ss,
    g_rs,
    on_ss,
    on_rs,
    rp_ss,
    rp_rs,
    rk_ss,
    rk_rs,
):
    me = Where(n_ctx, n_fsdp)
    share = me.share
    rows, width = x_ref.shape
    units = wgu_ref.shape[1] // 2
    per = units // 128
    blocks = TENSOR * per // n_fsdp
    enter([me.partner] + [me.peer(k) for k in range(1, share)])
    sends = []

    def start(copy):
        copy.start()
        sends.append(copy)
        return copy

    plane = Plane(me, start)
    half_rows = pl.ds(pl.multiple_of(me.h * QCOLS, 64), QCOLS)
    own_out = ob_ref[...].reshape(2 * rows, WIDE)[:, :QCOLS]
    mix[...] = dot(own_out, wo_ref[half_rows, :]).reshape(2, rows, width)
    mixed = start(remote(mix.at[1 - me.h], mix_in, pair_ss.at[0], pair_rs.at[0], me.partner))
    for j in range(per):
        block = (me.t + TENSOR * j) // blocks
        wd[128 * j : 128 * (j + 1), :] = wd_ref[block]
    gain = gain_ref[...]
    mixed.wait_recv()
    middle[...] = x_ref[...].astype(F32) + mix[me.h] + mix_in[...]

    def scaled_of():
        h = middle[...]
        inverse = lax.rsqrt(jnp.mean(h * h, axis=-1, keepdims=True) + epsilon)
        return h * inverse, inverse

    n2[...] = (scaled_of()[0] * gain).astype(BF)
    n2_all[me.t] = n2[...]

    def sems(phase):
        return (
            pair_ss.at[1 + phase],
            pair_rs.at[1 + phase],
            g_ss.at[phase],
            g_rs.at[phase],
            on_ss.at[phase],
            on_rs.at[phase],
        )

    def chip_rows(everything, k):
        first = lax.rem(2 * me.chip(k), TENSOR)
        return jnp.concatenate([everything[first], everything[first + 1]], axis=0)

    def reduce_start(phase, k):
        pair_out[phase, k] = wide[1 - me.h].astype(BF)
        keep[k] = wide[me.h]
        return start(
            remote(
                pair_out.at[phase, k],
                pair_in.at[phase, k],
                rp_ss.at[phase, k],
                rp_rs.at[phase, k],
                me.partner,
            )
        )

    def reduce_on(phase, k, copy):
        copy.wait_recv()
        both = keep[k] + pair_in[phase, k].astype(F32)
        if k == 0:
            keep[0] = both
            return None
        peer_out[phase, k] = both.astype(BF)
        return start(
            remote(
                peer_out.at[phase, k],
                peer_in.at[phase, k],
                rk_ss.at[phase, k],
                rk_rs.at[phase, k],
                me.peer(k),
            )
        )

    def gathered(phase, own, everything, work):
        copies = plane.gather_start(own, everything, sems(phase))
        copies[0].wait_recv()
        first = None
        ons, parts, peers = {}, {}, {}
        work(0)
        parts[0] = reduce_start(phase, 0)
        for k in range(1, share):
            ons[k] = plane.pass_on(k, copies, everything, sems(phase))
        for k in range(1, share):
            ons[k].wait_recv()
            work(k)
            parts[k] = reduce_start(phase, k)
            if k > 1:
                peers[k - 1] = reduce_on(phase, k - 1, parts[k - 1])
        peers[share - 1] = reduce_on(phase, share - 1, parts[share - 1])
        reduce_on(phase, 0, parts[0])
        return peers

    def summed(phase, peers):
        result = keep[0]
        for k in range(1, share):
            peers[k].wait_recv()
            result = result + peer_in[phase, k].astype(F32)
        return result

    def forward(k):
        both = dot(chip_rows(n2_all, k), wgu_ref[...])
        gate, up = both[:, :units], both[:, units:]
        gate_s[k], up_s[k] = gate, up
        inner = (gate * jax.nn.sigmoid(gate) * up).astype(BF)
        inner_s[k] = inner
        wide[...] = dot(inner, wd[...]).reshape(2, rows, width)

    peers = gathered(0, n2, n2_all, forward)
    final = middle[...] + summed(0, peers)
    total_rows = rows * n_ctx * n_fsdp
    factor = total_rows / count_ref[0:1, 0:1] * valid_ref[...]
    grad_final = factor * (final - teacher_ref[...].astype(F32))
    dy_s[...] = grad_final
    dyb[...] = grad_final.astype(BF)
    dyb_all[me.t] = dyb[...]

    def backward(k):
        grad_inner = dot_t(chip_rows(dyb_all, k), wd[...])
        gate, up = gate_s[k], up_s[k]
        sigma = jax.nn.sigmoid(gate)
        grad_gate = (grad_inner * up * sigma * (1.0 + gate * (1.0 - sigma))).astype(BF)
        grad_up = (grad_inner * gate * sigma).astype(BF)
        dgu_s[k, :, :units] = grad_gate
        dgu_s[k, :, units:] = grad_up
        wide[...] = dot_t(dgu_s[k], wgu_ref[...]).reshape(2, rows, width)

    peers = gathered(1, dyb, dyb_all, backward)

    def each_chip(everything):
        return jnp.concatenate([chip_rows(everything, k) for k in range(share)], axis=0)

    tall = 2 * rows * share
    grads = dgu_s[...].reshape(tall, 2 * units)
    inner_all = inner_s[...].reshape(tall, units)
    step = 128
    for j in range(width // step):
        cols = slice(step * j, step * (j + 1))
        tokens = jnp.concatenate([n2_all[lax.rem(2 * me.chip(k), TENSOR) + e, :, cols] for k in range(share) for e in range(2)], axis=0)
        gwgu_ref[cols, :] = t_dot(tokens, grads).astype(BF)
    for d in range(n_fsdp):
        gwd_ref[d] = jnp.zeros((128, width), BF)
    dy_tokens = each_chip(dyb_all)
    for j in range(per):
        block = (me.t + TENSOR * j) // blocks
        gwd_ref[block] = t_dot(inner_all[:, 128 * j : 128 * (j + 1)], dy_tokens).astype(BF)

    grad_normed = summed(1, peers)
    scaled, inverse = scaled_of()
    weighted = grad_normed * gain
    ggain_ref[...] = jnp.broadcast_to(
        jnp.sum(grad_normed * scaled, axis=0, keepdims=True), (8, width)
    )
    grad_middle = dy_s[...] + inverse * (
        weighted - scaled * jnp.mean(weighted * scaled, axis=-1, keepdims=True)
    )
    gm_ref[...] = grad_middle
    dhb_all[me.h] = grad_middle.astype(BF)
    swapped = start(
        remote(dhb_all.at[me.h], dhb_all.at[me.h], pair_ss.at[3], pair_rs.at[3], me.partner)
    )
    swapped.wait_recv()
    grad_out = dhb_all[...].reshape(2 * rows, width)
    dob = dot_t(grad_out, wo_ref[half_rows, :]).astype(BF)
    dob_ref[...] = jnp.zeros(dob_ref.shape, BF)
    for core in range(2):
        dob_ref[core, :, :QCOLS] = dob[core * rows : (core + 1) * rows]
    gwo_ref[...] = jnp.zeros(gwo_ref.shape, BF)
    gwo_ref[half_rows, :] = t_dot(own_out, grad_out).astype(BF)
    for copy in sends:
        copy.wait_send()


def feed_call(n_ctx, n_fsdp, x, ob, wo, wgu, wd, gain, teacher, valid, count):
    rows, width = x.shape
    share = TENSOR // 2
    units = wgu.shape[1] // 2
    vmem = pl.BlockSpec(memory_space=pltpu.VMEM)
    dma = pltpu.SemaphoreType.DMA
    outs = (
        jax.ShapeDtypeStruct((rows, width), F32),
        jax.ShapeDtypeStruct((2, rows, WIDE), BF),
        jax.ShapeDtypeStruct((HQ * HD, width), BF),
        jax.ShapeDtypeStruct((width, 2 * units), BF),
        jax.ShapeDtypeStruct((n_fsdp, 128, width), BF),
        jax.ShapeDtypeStruct((8, width), F32),
    )
    block = (rows, width)
    return pl.pallas_call(
        functools.partial(feed_kernel, n_ctx, n_fsdp),
        out_shape=outs,
        in_specs=[vmem] * 9,
        out_specs=(vmem,) * len(outs),
        scratch_shapes=[
            pltpu.VMEM((2,) + block, F32),
            pltpu.VMEM(block, F32),
            pltpu.VMEM(block, F32),
            pltpu.VMEM(block, BF),
            pltpu.VMEM((TENSOR,) + block, BF),
            pltpu.VMEM((units, width), BF),
            pltpu.VMEM((share, 2 * rows, units), F32),
            pltpu.VMEM((share, 2 * rows, units), F32),
            pltpu.VMEM((share, 2 * rows, units), BF),
            pltpu.VMEM((share, 2 * rows, 2 * units), BF),
            pltpu.VMEM((2,) + block, F32),
            pltpu.VMEM((share,) + block, F32),
            pltpu.VMEM((2, share) + block, BF),
            pltpu.VMEM((2, share) + block, BF),
            pltpu.VMEM((2, share) + block, BF),
            pltpu.VMEM((2, share) + block, BF),
            pltpu.VMEM(block, F32),
            pltpu.VMEM(block, BF),
            pltpu.VMEM((TENSOR,) + block, BF),
            pltpu.VMEM((2,) + block, BF),
            dma((4,)),
            dma((4,)),
        ]
        + [dma((2, share))] * 8,
        compiler_params=pltpu.CompilerParams(
            collective_id=2, has_side_effects=True, vmem_limit_bytes=60 * 2**20
        ),
        cost_estimate=pl.CostEstimate(
            flops=9 * 10**9, bytes_accessed=20 * 2**20, transcendentals=10**6
        ),
        name="feed_forward",
    )(x, ob, wo, wgu, wd, gain, teacher, valid, count)


def backward_kernel(
    n_ctx,
    n_fsdp,
    x_ref,
    ob_ref,
    dob_ref,
    lse_ref,
    qs_ref,
    kv_ref,
    wf_ref,
    n1_ref,
    gm_ref,
    gains_ref,
    ggain_ref,
    cos_ref,
    sin_ref,
    starts_ref,
    gi_ref,
    gw_ref,
    gsum_ref,
    bias,
    dos,
    delta,
    qdt,
    dq,
    acc,
    dk_out,
    dk_in,
    kz_out,
    kz_in,
    n1_all,
    dqs,
    dqa,
    mix,
    mix_in,
    dw,
    dw_out,
    dw_in,
    gs_s,
    gs_r,
    pair_ss,
    pair_rs,
    kp_ss,
    kp_rs,
    kz_ss,
    kz_rs,
    n_ss,
    n_rs,
    on_ss,
    on_rs,
    qa_ss,
    qa_rs,
    wz_ss,
    wz_rs,
    gp_ss,
    gp_rs,
    gz_ss,
    gz_rs,
    wp_ss,
    wp_rs,
    wo_ss,
    wo_rs,
):
    me = Where(n_ctx, n_fsdp)
    chips, share = me.chips, me.share
    rows, width = x_ref.shape
    depth = width // n_fsdp
    piece = PACKED // share
    stacked = STACK * 128
    n_keys = n_fsdp * 128
    enter(
        [me.partner]
        + [me.line(d) for d in range(1, n_fsdp)]
        + [me.peer(k) for k in range(1, chips)]
    )
    sends = []

    def start(copy):
        copy.start()
        sends.append(copy)
        return copy

    low = low_lanes((2 * rows, 128))
    for i in range(WIDE // 128):
        cols = slice(128 * i, 128 * (i + 1))
        grads = dob_ref[:, :, cols].reshape(2 * rows, 128).astype(F32)
        outs = ob_ref[:, :, cols].reshape(2 * rows, 128).astype(F32)
        for odd in range(2):
            head = 2 * i + odd
            if head == GROUPS * STACK:
                continue
            g, j = head // STACK, head % STACK
            mine = jnp.where(low, 0.0 if odd else grads, grads if odd else 0.0)
            dots = jnp.sum(mine * outs, axis=-1, keepdims=True)
            if not odd:
                mine = pltpu.roll(mine, HD, 1)
            mine = mine.astype(BF)
            for half in range(2):
                for core in range(2):
                    source = slice(core * rows + half * 64, core * rows + half * 64 + 64)
                    target = slice(j * 128 + core * 64, j * 128 + core * 64 + 64)
                    dos[g, half, target, :] = mine[source]
                    delta[g, half, target, :] = dots[source]
    for g in range(GROUPS):
        for half in range(2):
            qdt[g, half, :, :stacked] = qs_ref[g, half].T
            qdt[g, half, :, stacked:] = dos[g, half].T
    dq[...] = jnp.zeros(dq.shape, F32)

    def chunk(query_half, key_half, chip):
        bias[...] = bias_of(me, starts_ref, query_half, key_half, chip)

        def group(g, unused):
            kv = kv_ref[g, key_half, chip]
            scores = dot_t(qs_ref[g, query_half], kv) * (0.125 * LOG2E)
            scores = (scores.reshape(STACK, 128, n_keys) + bias[...][None]).reshape(
                stacked, n_keys
            )
            probs = jnp.exp2(scores - lse_ref[g, query_half][:, 0:1])
            grad_probs = dot_t(dos[g, query_half], kv)
            grad_scores = (0.125 * probs * (grad_probs - delta[g, query_half])).astype(BF)
            dq[g, query_half] += dot(grad_scores, kv)
            both = jnp.concatenate([grad_scores, probs.astype(BF)], axis=0)
            acc[g, key_half] += dot(qdt[g, query_half], both)
            return unused

        lax.fori_loop(0, GROUPS, group, 0)

    kp = {}
    slots = dk_out.shape[0]
    for k in range(chips - 1, -1, -1):
        chip = me.chip(k)
        high = (chip >= me.p).astype(jnp.int32)
        acc[...] = jnp.zeros(acc.shape, F32)
        chunk(1, 0, chip)
        chunk(high, high, chip)
        if k:
            if k + slots < chips:
                kp[k + slots].wait_send()
            dk_out[k % slots] = acc[...].astype(BF)
            kp[k] = remote(
                dk_out.at[k % slots], dk_in.at[k - 1], kp_ss.at[k], kp_rs.at[k], me.peer(k)
            )
            kp[k].start()
        else:
            chunk(0, 0, chip)
    for k in range(1, min(slots + 1, chips)):
        sends.append(kp[k])

    n1_all[me.t] = n1_ref[me.h]
    n1_all[me.t + 1 - 2 * me.h] = n1_ref[1 - me.h]
    ng = {}
    for k in range(1, share):
        slot = n1_all.at[me.t]
        ng[k] = start(remote(n1_ref.at[me.h], slot, n_ss.at[k], n_rs.at[k], me.peer(k)))

    cosine, sine = cos_ref[...], -sin_ref[...]

    def by_core(pieces, cut):
        return jnp.concatenate(
            [pieces[half][cut + core * 64 : cut + core * 64 + 64] for core in range(2) for half in range(2)],
            axis=0,
        )

    def query_grad(head):
        g, j = head // STACK, head % STACK
        return by_core([dq[g, 0], dq[g, 1]], j * 128)

    def put(i, tile):
        per = piece // 128
        dqs[i // per, :, 128 * (i % per) : 128 * (i % per + 1)] = tile.astype(BF)

    for i in range(4):
        tile = jnp.where(low, query_grad(2 * i), pltpu.roll(query_grad(2 * i + 1), HD, 1))
        put(i, turn(tile, cosine, sine))
    last_query = query_grad(8)

    for k in range(chips - 1, 0, -1):
        kp[k].wait_recv()
    for g in range(GROUPS):
        for half in range(2):
            value = acc[g, half]
            for k in range(1, chips):
                value = value + dk_in[k - 1, g, half].astype(F32)
            acc[g, half] = value
    kz = {}
    for d in range(1, n_fsdp):
        cols = pl.ds(pl.multiple_of(flip(me.z, d) * 128, 128), 128)
        kz_out[d] = acc[:, :, :, cols].astype(BF)
        kz[d] = start(remote(kz_out.at[d], kz_in.at[d], kz_ss.at[d], kz_rs.at[d], me.line(d)))
    ons = {}
    for k in range(1, share):
        ng[k].wait_recv()
        slot = n1_all.at[lax.rem(2 * me.chip(k) + me.h, TENSOR)]
        ons[k] = start(remote(slot, slot, on_ss.at[k], on_rs.at[k], me.partner))
    for d in range(1, n_fsdp):
        kz[d].wait_recv()
    own_cols = pl.ds(pl.multiple_of(me.z * 128, 128), 128)
    pairs = []
    for g in range(GROUPS):
        halves = []
        for half in range(2):
            value = acc[g, half, :, own_cols]
            for d in range(1, n_fsdp):
                value = value + kz_in[d, g, half].astype(F32)
            halves.append(value.T)
        pairs.append(by_core(halves, 0))
    moved = [pltpu.roll(pair, HD, 1) for pair in pairs]
    put(4, turn(jnp.where(low, last_query, moved[0]), cosine, sine))
    put(5, turn(jnp.where(low, pairs[1], moved[2]), cosine, sine))
    put(6, jnp.where(low, moved[0], pairs[1]))
    put(7, jnp.where(low, moved[2], 0.0))

    qa = {}
    for k in range(1, share):
        qa[k] = start(
            remote(
                dqs.at[lax.rem(me.chip(k), share)],
                dqa.at[k],
                qa_ss.at[k],
                qa_rs.at[k],
                me.peer(k),
            )
        )
    dqa[0] = dqs[me.s]
    whole = dot_t(dqs[0], wf_ref[:, :piece])
    for i in range(1, share):
        whole = whole + dot_t(dqs[i], wf_ref[:, piece * i : piece * (i + 1)])
    mix[...] = whole.reshape(2, rows, width)
    mixed = start(remote(mix.at[1 - me.h], mix_in, pair_ss.at[0], pair_rs.at[0], me.partner))
    for k in range(1, share):
        ons[k].wait_recv()
        qa[k].wait_recv()
    tall = 2 * rows * share
    grads = dqa[...].reshape(tall, piece)
    for j in range(width // 128):
        cols = slice(128 * j, 128 * (j + 1))
        tokens = jnp.concatenate(
            [
                n1_all[lax.rem(2 * me.chip(k), TENSOR) + e, :, cols]
                for k in range(share)
                for e in range(2)
            ],
            axis=0,
        )
        dw[cols, :] = t_dot(tokens, grads)
    wz = {}
    for d in range(1, n_fsdp):
        dw_out[d] = dw[pl.ds(pl.multiple_of(flip(me.z, d) * depth, 16), depth), :].astype(BF)
        wz[d] = start(remote(dw_out.at[d], dw_in.at[d], wz_ss.at[d], wz_rs.at[d], me.line(d)))

    mixed.wait_recv()
    grad_normed = mix[me.h] + mix_in[...]
    x = x_ref[...].astype(F32)
    inverse = lax.rsqrt(jnp.mean(x * x, axis=-1, keepdims=True) + epsilon)
    scaled = x * inverse
    gs_s[0, 0:1] = jnp.sum(grad_normed * scaled, axis=0, keepdims=True)
    gs_s[0, 1:8] = ggain_ref[1:8]
    gain_pair = start(remote(gs_s.at[0], gs_r.at[0], pair_ss.at[1], pair_rs.at[1], me.partner))
    weighted = grad_normed * gains_ref[0:1]
    gi_ref[...] = gm_ref[...] + inverse * (
        weighted - scaled * jnp.mean(weighted * scaled, axis=-1, keepdims=True)
    )
    gain_pair.wait_recv()
    gs_s[1] = gs_s[0] + gs_r[0]
    gp = [
        start(remote(gs_s.at[1], gs_r.at[k], gp_ss.at[k], gp_rs.at[k], me.peer(k)))
        for k in range(1, chips)
    ]
    for d in range(1, n_fsdp):
        wz[d].wait_recv()
    value = dw[pl.ds(pl.multiple_of(me.z * depth, 16), depth), :]
    for d in range(1, n_fsdp):
        value = value + dw_in[d].astype(F32)
    gw_ref[me.c] = value.astype(BF)
    wp = {}
    own = gw_ref.at[me.c]
    for k in range(1, chips):
        wp[k] = start(remote(own, own, wp_ss.at[k], wp_rs.at[k], me.peer(k)))
    last = [start(remote(own, own, wo_ss.at[0], wo_rs.at[0], me.partner))]
    plane_sum = gs_s[1]
    for k in range(1, chips):
        gp[k - 1].wait_recv()
        plane_sum = plane_sum + gs_r[k]
    gs_s[2] = plane_sum
    gz = [
        start(remote(gs_s.at[2], gs_r.at[chips + d], gz_ss.at[d], gz_rs.at[d], me.line(d)))
        for d in range(1, n_fsdp)
    ]
    for k in range(1, chips):
        wp[k].wait_recv()
        slot = gw_ref.at[2 * me.chip(k) + me.h]
        last.append(start(remote(slot, slot, wo_ss.at[k], wo_rs.at[k], me.partner)))
    for d in range(1, n_fsdp):
        gz[d - 1].wait_recv()
        plane_sum = plane_sum + gs_r[chips + d]
    gsum_ref[...] = plane_sum
    for copy in last:
        copy.wait_recv()
    for copy in sends:
        copy.wait_send()


def backward_call(
    n_ctx, n_fsdp, x, ob, dob, lse, qs, kv, wf, n1, gm, gains, ggain, cosine, sine, starts
):
    rows, width = x.shape
    chips, share = n_ctx // 2, TENSOR // 2
    keys = n_fsdp * 128
    stacked = STACK * 128
    depth = width // n_fsdp
    piece = PACKED // share
    vmem = pl.BlockSpec(memory_space=pltpu.VMEM)
    dma = pltpu.SemaphoreType.DMA
    block = (rows, width)
    outs = (
        jax.ShapeDtypeStruct(block, F32),
        jax.ShapeDtypeStruct((n_ctx, depth, piece), BF),
        jax.ShapeDtypeStruct((8, width), F32),
    )
    return pl.pallas_call(
        functools.partial(backward_kernel, n_ctx, n_fsdp),
        out_shape=outs,
        in_specs=[vmem] * 13 + [pl.BlockSpec(memory_space=pltpu.SMEM)],
        out_specs=(vmem,) * len(outs),
        scratch_shapes=[
            pltpu.VMEM((128, keys), F32),
            pltpu.VMEM((GROUPS, 2, stacked, 128), BF),
            pltpu.VMEM((GROUPS, 2, stacked, 1), F32),
            pltpu.VMEM((GROUPS, 2, 128, 2 * stacked), BF),
            pltpu.VMEM((GROUPS, 2, stacked, 128), F32),
            pltpu.VMEM((GROUPS, 2, 128, keys), F32),
            pltpu.VMEM((min(chips - 1, 4), GROUPS, 2, 128, keys), BF),
            pltpu.VMEM((chips - 1, GROUPS, 2, 128, keys), BF),
            pltpu.VMEM((n_fsdp, GROUPS, 2, 128, 128), BF),
            pltpu.VMEM((n_fsdp, GROUPS, 2, 128, 128), BF),
            pltpu.VMEM((TENSOR,) + block, BF),
            pltpu.VMEM((share, 2 * rows, piece), BF),
            pltpu.VMEM((share, 2 * rows, piece), BF),
            pltpu.VMEM((2,) + block, F32),
            pltpu.VMEM(block, F32),
            pltpu.VMEM((width, piece), F32),
            pltpu.VMEM((n_fsdp, depth, piece), BF),
            pltpu.VMEM((n_fsdp, depth, piece), BF),
            pltpu.VMEM((3, 8, width), F32),
            pltpu.VMEM((chips + n_fsdp, 8, width), F32),
            dma((2,)),
            dma((2,)),
            dma((chips,)),
            dma((chips,)),
            dma((n_fsdp,)),
            dma((n_fsdp,)),
            dma((share,)),
            dma((share,)),
            dma((share,)),
            dma((share,)),
            dma((share,)),
            dma((share,)),
            dma((n_fsdp,)),
            dma((n_fsdp,)),
            dma((chips,)),
            dma((chips,)),
            dma((n_fsdp,)),
            dma((n_fsdp,)),
            dma((chips,)),
            dma((chips,)),
            dma((chips,)),
            dma((chips,)),
        ],
        compiler_params=pltpu.CompilerParams(
            collective_id=3, has_side_effects=True, vmem_limit_bytes=60 * 2**20
        ),
        cost_estimate=pl.CostEstimate(
            flops=9 * 10**9, bytes_accessed=20 * 2**20, transcendentals=6 * 10**6
        ),
        name="attention_backward",
    )(x, ob, dob, lse, qs, kv, wf, n1, gm, gains, ggain, cosine, sine, starts)


def tables(n_ctx, n_fsdp, rows):
    chip = lax.axis_index("ctx") // 2
    fsdp_slot = lax.axis_index("fsdp")
    index = jnp.arange(2 * rows, dtype=jnp.int32)
    slot = 2 * chip + index // rows
    within = index % rows
    half_rows = rows // 2
    slab = jnp.where(within < half_rows, slot, 2 * n_ctx - 1 - slot)
    places = slab * (n_fsdp * half_rows) + fsdp_slot * half_rows + within % half_rows
    half_size = HD // 2
    frequency = rope_base ** (-2.0 * jnp.arange(half_size, dtype=jnp.float32) / HD)
    angles = places.astype(F32)[:, None] * frequency[None, :]
    cosine, sine = jnp.cos(angles), jnp.sin(angles)
    return (
        jnp.concatenate([cosine] * 4, axis=1),
        jnp.concatenate([-sine, sine, -sine, sine], axis=1),
    )


def per_device(
    hidden_in,
    attention_gain,
    query_weight,
    key_weight,
    value_weight,
    out_weight,
    feed_gain,
    gate_weight,
    up_weight,
    down_weight,
    teacher,
    valid_mask,
    doc_starts,
):
    n_ctx = lax.axis_size("ctx")
    n_fsdp = lax.axis_size("fsdp")
    rows, width = hidden_in.shape
    depth = query_weight.shape[0]
    ff = gate_weight.shape[1]
    ctx = lax.axis_index("ctx")
    slot = lax.axis_index("fsdp")
    second = ctx % 2 == 1
    t = ctx % TENSOR
    per = ff // 128 // TENSOR
    blocks = ff // 128 // n_fsdp

    def half_of(weight, cols):
        return jnp.where(second, weight[:, cols:], weight[:, :cols])

    packed = jnp.concatenate(
        [
            half_of(query_weight, QCOLS),
            half_of(key_weight, KCOLS),
            half_of(value_weight, KCOLS),
            attention_gain[:, None],
            feed_gain[:, None],
            jnp.zeros((depth, PACKED - QCOLS - 2 * KCOLS - 2), BF),
        ],
        axis=1,
    )
    wo = lax.all_gather(out_weight, "fsdp", axis=0, tiled=True)

    def own_units(weight):
        shaped = weight.reshape(depth, per, TENSOR, 128)
        return lax.dynamic_index_in_dim(shaped, t, 2, keepdims=False).reshape(depth, per * 128)

    wgu = lax.all_gather(
        jnp.concatenate([own_units(gate_weight), own_units(up_weight)], axis=1),
        "fsdp",
        axis=0,
        tiled=True,
    )
    turn_of = (t - blocks * slot) % TENSOR
    shaped = down_weight.reshape(blocks, 128, width)
    candidate = lax.dynamic_index_in_dim(
        shaped, jnp.minimum(turn_of, blocks - 1), 0, keepdims=False
    )
    wd = lax.all_gather(candidate, "fsdp", axis=0)

    cosine, sine = tables(n_ctx, n_fsdp, rows)
    ob, lse, qs, kv, wf, n1, gains, count = forward_call(
        n_ctx, n_fsdp, hidden_in, packed, cosine, sine, valid_mask.reshape(1, rows), doc_starts
    )
    gm, dob, gwo, gwgu, gwd, ggain = feed_call(
        n_ctx,
        n_fsdp,
        hidden_in,
        ob,
        wo,
        wgu,
        wd,
        gains[1:2],
        teacher,
        valid_mask.astype(F32).reshape(rows, 1),
        count,
    )
    own_gu = lax.psum_scatter(gwgu, "fsdp", scatter_dimension=0, tiled=True)
    own_d = lax.psum_scatter(gwd.reshape(-1, width), "fsdp", scatter_dimension=0, tiled=True)
    own_o = lax.psum_scatter(gwo, "fsdp", scatter_dimension=0, tiled=True)

    def over_groups(value):
        value = value.reshape((n_ctx // TENSOR, TENSOR) + value.shape[1:])
        return jnp.sum(value.astype(F32), axis=0)

    all_gu = over_groups(lax.all_gather(own_gu, "ctx", axis=0))
    all_d = over_groups(lax.all_gather(own_d, "ctx", axis=0))
    grad_out = lax.psum(own_o, "ctx").astype(F32)
    gi, gw, gsum = backward_call(
        n_ctx,
        n_fsdp,
        hidden_in,
        ob,
        dob,
        lse,
        qs,
        kv,
        wf,
        n1,
        gm,
        gains,
        ggain,
        cosine,
        sine,
        doc_starts,
    )

    def unit_grads(value):
        return (
            value.reshape(TENSOR, depth, per, 128).transpose(1, 2, 0, 3).reshape(depth, ff)
        )

    grad_gate = unit_grads(all_gu[:, :, : per * 128])
    grad_up = unit_grads(all_gu[:, :, per * 128 :])
    turns = (blocks * slot + jnp.arange(blocks)) % TENSOR
    grad_down = jnp.take(all_d, turns, axis=0).reshape(blocks * 128, width)
    packed_grads = over_groups(gw).reshape(TENSOR // 2, 2, depth, -1).transpose(1, 2, 0, 3)
    packed_grads = packed_grads.reshape(2, depth, PACKED)

    def both(first, cols):
        return jnp.concatenate(
            [packed_grads[0, :, first : first + cols], packed_grads[1, :, first : first + cols]],
            axis=1,
        )

    own_gains = lax.dynamic_slice_in_dim(gsum[:2], slot * depth, depth, axis=1)
    return (
        gi,
        own_gains[0],
        both(0, QCOLS),
        both(QCOLS, KCOLS),
        both(QCOLS + KCOLS, KCOLS),
        grad_out,
        own_gains[1],
        grad_gate,
        grad_up,
        grad_down,
    )


def solution(mesh):
    token = P(("ctx", "fsdp"), None)
    weight = P("fsdp", None)
    gain = P("fsdp")
    in_specs = (
        (token, gain)
        + (weight,) * 4
        + (gain,)
        + (weight,) * 3
        + (token, P(("ctx", "fsdp")), P())
    )
    out_specs = (token, gain) + (weight,) * 4 + (gain,) + (weight,) * 3
    return jax.shard_map(
        per_device, mesh=mesh, in_specs=in_specs, out_specs=out_specs, check_vma=False
    )
```
